32 devices in a mesh: dp: 4 (over z), section: 2 (over core), tensor: 4 (over y, x).
Axes of the slice: x: 2, y: 2, z: 4, core: 2. Of those that a mesh axis runs over, the one named last changes fastest.
Arguments:
- tokens: bfloat16 [8, 128, 4096], P('dp', 'tensor'), may hold values from -6 to 6
- segment: int32 [8, 128], P('dp'), may hold values from 0 to 3, never falling along the last dimension, each value on 1 to 64 neighbouring positions
- pack_source: int32 [8], P('dp'), may hold values from 0 to 7, as said below
- norm_gain: float32 [2, 4096], P('section'), may hold values from 0.1 to 1.9
- qkv_weight: bfloat16 [2, 4096, 6144], P('section', None, 'tensor'), may hold values from -3 to 3
- out_weight: bfloat16 [2, 4096, 4096], P('section', 'tensor'), may hold values from -0.1875 to 0.1875
Outputs:
- final_hidden: bfloat16 [8, 128, 4096], P('dp', 'tensor', 'section')
The draws below stay inside these ranges and needn't reach their ends.
Inputs may be any that keep to these rules, and one draw needn't show every extreme that they name: segment numbers never fall along a pack; each response covers 1 to 64 positions. `pack_source`: each pack number appears once; the 2 slots of one index of dp take packs held by 2 different indices of dp, and the 2 packs held by one index of dp go to slots of 2 different indices of dp.
All inputs are finite; a program needn't handle non-finite values.
Results may differ from the reference program's by a relative error of at most 0.017.
Values may be sent and summed in bfloat16 or wider, within the bound.
A program may use at most 128 MiB of HBM per device.

```python
import math
import jax
import jax.numpy as jnp
import numpy as np
from jax import lax

D = 4096
HQ = 32
KVH = 8
HD = 128
GROUP = 4
PACK = 128
SEGS = 4
MB = 2
LAYERS = 2
PACKS = 8
N_TENSOR = 4


def draw_qkv_weight(key, part):
    key = jax.random.fold_in(key, 11)
    weights_base = jax.random.truncated_normal(key, -6.0, 6.0, (LAYERS, D, KVH, GROUP + 2, HD), jnp.float32) * D ** (-0.5)
    return weights_base.reshape(LAYERS, D, KVH * (GROUP + 2) * HD).astype(jnp.bfloat16)


def place_value(order, position, wanted):
    found = jnp.argmax((order == wanted).astype(jnp.int32)).astype(jnp.int32)
    current = order[position]
    order = order.at[found].set(current)
    return order.at[position].set(wanted)


def draw_pack_source(key, part):
    key = jax.random.fold_in(key, 23)
    holders = PACKS // MB
    order = jax.random.permutation(jax.random.fold_in(key, 1), holders).astype(jnp.int32)
    anchor = jax.random.randint(jax.random.fold_in(key, 4), (), 0, holders).astype(jnp.int32)
    order = place_value(order, anchor, (anchor + holders // 2) % holders)
    order = place_value(order, (anchor + 1) % holders, anchor)
    extra = jax.random.permutation(jax.random.fold_in(key, 2), holders - 1).astype(jnp.int32)[:MB - 1] + 1
    offsets = jnp.concatenate([jnp.zeros((1,), jnp.int32), extra])
    takers = jnp.arange(holders, dtype=jnp.int32)
    holder = (order[takers][:, None] + offsets[None, :]) % holders
    scores = jax.random.randint(jax.random.fold_in(key, 3), (holders, MB), 0, 1 << 20) * MB + jnp.arange(MB, dtype=jnp.int32)[None, :]
    local_order = jnp.argsort(scores, axis=1, stable=True).astype(jnp.int32)
    slot_index = jnp.broadcast_to(jnp.arange(MB, dtype=jnp.int32)[None, :], (holders, MB))
    local = local_order[holder, slot_index]
    return (holder * MB + local).reshape(PACKS).astype(jnp.int32)


def level_of(stream_key, shape, shards, least, high):
    level, own = 1.0, jax.random.fold_in(stream_key, 6)
    for dim, shards_of in shards:
        draws = jnp.exp(jax.random.uniform(jax.random.fold_in(own, dim), (shards_of,), jnp.float32, least / len(shards), high / len(shards)))
        level = level * jnp.repeat(draws, shape[dim] // shards_of).reshape([-1 if axis == dim else 1 for axis in range(len(shape))])
    return level


def split_up(count, total, limit, slope):
    loads = [(1 << 20) // math.isqrt(rank ** slope) + 1 for rank in range(2, count + 1)]
    surplus, given = total - limit - (count - 1), [1] * (count - 1)
    while surplus > 0:
        candidates = [i for i in range(count - 1) if given[i] < limit]
        mass, budget = sum([loads[i] for i in candidates]), surplus
        for i in candidates:
            addition = min(limit - given[i], max(1, budget * loads[i] // mass), surplus)
            given[i] = given[i] + addition
            surplus = surplus - addition
    return np.array([limit] + given)


def uneven(own_key, count, total, most, skew):
    if count == 2:
        one = jax.random.randint(own_key, (), max(1, total - most), min(most, total - 1) + 1)
        return jnp.stack([one, total - one])
    lengths = jnp.asarray(split_up(count, total, most, skew), jnp.int32)
    pairs = (count - 1) // 2
    source_of, sink = lengths[1:1 + 2 * pairs:2], lengths[2:2 + 2 * pairs:2]
    margin = jnp.minimum(source_of - 1, most - sink)
    moved = jax.random.randint(jax.random.fold_in(own_key, 1), (pairs,), 0, 1 << 20) % (margin + 1)
    lengths = lengths.at[1:1 + 2 * pairs:2].set(source_of - moved).at[2:2 + 2 * pairs:2].set(sink + moved)
    return lengths[jax.random.permutation(jax.random.fold_in(own_key, 2), count)]


def scatter_about(own_key, shape, width, bound, split=(), held_as=jnp.bfloat16):
    level = level_of(own_key, shape, split, -0.22, 0.18) if split else 1.0
    entries = jax.random.normal(own_key, shape, jnp.float32) * width * level
    return jnp.minimum(jnp.maximum(entries, -bound), bound).astype(held_as)


def setup_inputs(seed: int = 0) -> dict:
    splits = jax.random.split(jax.random.key(seed), 7)
    return {
        "tokens": scatter_about(splits[0], (PACKS, PACK, D), 1.0, 6.0, ((0, 4), (1, 4))),
        "segment": jax.vmap(lambda own: jnp.searchsorted(jnp.cumsum(uneven(own, SEGS, PACK, PACK // 2, 2)), jnp.arange(PACK), side="right"))(jax.random.split(splits[1], PACKS)).reshape((PACKS, PACK)).astype(jnp.int32),
        "pack_source": draw_pack_source(jax.random.fold_in(splits[6], 71), 0),
        "norm_gain": jnp.clip(1.0 + 0.18 * jax.random.normal(splits[3], (LAYERS, D), jnp.float32), 0.1, 1.9),
        "qkv_weight": draw_qkv_weight(jax.random.fold_in(splits[6], 71), 0),
        "out_weight": scatter_about(splits[5], (LAYERS, HQ * HD, D), (HQ * HD // 4) ** -0.5, 0.1875, ((0, 2), (1, 4))),
    }


EPSILON = 1e-05
ROPE_BASE = 500000.0

def rotate_pairs(values, cosine, sine_table):
    half_width = values.shape[-1] // 2
    first_half = values[..., :half_width]
    second_half = values[..., half_width:]
    return jnp.concatenate([first_half * cosine - second_half * sine_table, second_half * cosine + first_half * sine_table], axis=-1)

def rope_tables(segment_ids):
    length = segment_ids.shape[-1]
    earlier = lax.optimization_barrier(jnp.sum((segment_ids[..., None, :] < segment_ids[..., :, None]).astype(jnp.int32), axis=-1))
    position = (jnp.arange(length, dtype=jnp.int32) - earlier).astype(jnp.float32)
    exponent = jnp.arange(0, HD, 2, dtype=jnp.float32) / HD
    frequency = ROPE_BASE ** (-exponent)
    angles = position[..., None] * frequency
    return (jnp.cos(angles), jnp.sin(angles))

def rounded(values):
    return lax.optimization_barrier(values.astype(jnp.bfloat16)).astype(jnp.float32)

def attention_layer(hidden, allowed, cosine, sine_table, gain, weight_in, weight_out):
    mean_square = lax.optimization_barrier(jnp.mean(hidden * hidden, axis=-1, keepdims=True))
    normed = (hidden * lax.rsqrt(mean_square + EPSILON) * gain).astype(jnp.bfloat16)
    projected = jnp.dot(normed, weight_in, preferred_element_type=jnp.float32).reshape(PACK, KVH, GROUP + 2, HD)
    rotated = rotate_pairs(projected[:, :, :GROUP + 1], cosine[:, None, None, :], sine_table[:, None, None, :])
    qkv_rows = rounded(jnp.concatenate([rotated, projected[:, :, GROUP + 1:]], axis=2))
    queries = qkv_rows[:, :, :GROUP]
    keys_rows = qkv_rows[:, :, GROUP]
    values_rows = qkv_rows[:, :, GROUP + 1]
    scores = jnp.einsum('qkgd,skd->kgqs', queries, keys_rows) * HD ** (-0.5)
    scores = jnp.where(allowed, scores, -1e+30)
    largest = lax.optimization_barrier(jnp.max(scores, axis=-1, keepdims=True))
    exponent_terms = jnp.exp(scores - largest)
    weights = rounded(exponent_terms / lax.optimization_barrier(jnp.sum(exponent_terms, axis=-1, keepdims=True)))
    attended = rounded(jnp.einsum('kgqs,skd->qkgd', weights, values_rows))
    attended = attended.reshape(PACK, N_TENSOR, HQ * HD // N_TENSOR)
    blocks = weight_out.astype(jnp.float32).reshape(N_TENSOR, HQ * HD // N_TENSOR, D)
    partial_terms = rounded(jnp.einsum('pti,tid->tpd', attended, blocks))
    return lax.optimization_barrier(jnp.sum(partial_terms, axis=0))

def pack_forward(pack_tokens, pack_segments, norm_gain, qkv_weight, out_weight):
    cosine, sine_table = rope_tables(pack_segments)
    token_order = jnp.arange(PACK, dtype=jnp.int32)
    allowed = (pack_segments[:, None] == pack_segments[None, :]) & (token_order[None, :] <= token_order[:, None])
    hidden = pack_tokens.astype(jnp.float32)
    for layer_index in range(LAYERS):
        hidden = hidden + attention_layer(hidden, allowed, cosine, sine_table, norm_gain[layer_index], qkv_weight[layer_index], out_weight[layer_index])
    return hidden.astype(jnp.bfloat16)

def reference(tokens, segment, pack_source, norm_gain, qkv_weight, out_weight):
    selected = jnp.take(tokens, pack_source, axis=0)
    chosen = jnp.take(segment, pack_source, axis=0)
    return lax.map(lambda pack_pair: pack_forward(pack_pair[0], pack_pair[1], norm_gain, qkv_weight, out_weight), (selected, chosen))
```

```python
import functools

import jax
import jax.numpy as jnp
from jax import lax
from jax.experimental import pallas as pl
from jax.experimental.pallas import tpu as pltpu
from jax.sharding import PartitionSpec as P

HD = 128
GROUP = 4
EPSILON = 1e-05
ROPE_BASE = 500000.0
CHUNKS = 4
MESH = pl.DeviceIdType.MESH


def kernel(
    dp_count,
    tensor_count,
    frequency_ref,
    source_ref,
    segment_ref,
    tokens_ref,
    gain_ref,
    qkv_hbm,
    out_hbm,
    result_ref,
    weight_in,
    weight_out,
    meta,
    sent_packs,
    held_packs,
    gathered,
    hidden,
    hidden_low,
    normed,
    projected,
    square_sum,
    attended,
    partial,
    arrived,
    cosine,
    sine,
    bias,
    weight_sem,
    meta_send,
    meta_recv,
    pack_send,
    pack_recv,
    gather_send,
    gather_recv,
    next_send,
    sum_send,
    sum_recv,
):
    micro, rows, width = tokens_ref.shape
    length = segment_ref.shape[1]
    part = width // CHUNKS
    half = CHUNKS // 2
    z = lax.axis_index("dp")
    section = lax.axis_index("section")
    me = lax.axis_index("tensor")
    groups = weight_in.shape[2] // ((GROUP + 2) * HD)

    weight_copies = [
        pltpu.make_async_copy(
            qkv_hbm.at[0, pl.ds(c * part, part), :], weight_in.at[c], weight_sem.at[c]
        )
        for c in range(CHUNKS)
    ] + [
        pltpu.make_async_copy(
            out_hbm.at[0, :, pl.ds(c * part, part)], weight_out.at[c], weight_sem.at[CHUNKS + c]
        )
        for c in range(CHUNKS)
    ]
    for copy in weight_copies:
        copy.start()

    for i in range(micro):
        meta[z, i : i + 1, :] = segment_ref[i : i + 1, :]
        meta[z, micro + i : micro + i + 1, :] = jnp.full((1, length), source_ref[i], jnp.int32)

    barrier = pltpu.get_barrier_semaphore()

    @pl.loop(1, dp_count)
    def _(off):
        pl.semaphore_signal(
            barrier, inc=1, device_id={"dp": lax.rem(z + off, dp_count)}, device_id_type=MESH
        )

    for off in range(tensor_count):
        for other in range(2):
            if off == 0 and other == 0:
                continue
            pl.semaphore_signal(
                barrier,
                inc=1,
                device_id={
                    "tensor": lax.rem(me + off, tensor_count),
                    "section": lax.rem(section + other, 2),
                },
                device_id_type=MESH,
            )
    pl.semaphore_wait(barrier, dp_count - 1 + 2 * tensor_count - 1)

    def meta_copy(off):
        return pltpu.make_async_remote_copy(
            src_ref=meta.at[z],
            dst_ref=meta.at[z],
            send_sem=meta_send.at[off],
            recv_sem=meta_recv.at[off],
            device_id={"dp": lax.rem(z + off, dp_count)},
            device_id_type=MESH,
        )

    @pl.loop(1, dp_count)
    def _(off):
        meta_copy(off).start()

    @pl.loop(1, dp_count)
    def _(off):
        copy = meta_copy(off)
        copy.wait_send()
        copy.wait_recv()

    def pack_copy(c, off):
        target = lax.rem(z + off, dp_count)
        return pltpu.make_async_remote_copy(
            src_ref=sent_packs.at[c, target],
            dst_ref=held_packs.at[c, z],
            send_sem=pack_send.at[c, off],
            recv_sem=pack_recv.at[c, off],
            device_id={"dp": target},
            device_id_type=MESH,
        )

    def gather_copy(p, c, off):
        return pltpu.make_async_remote_copy(
            src_ref=gathered.at[p, c, pl.ds(pl.multiple_of(me * rows, rows), rows), :],
            dst_ref=gathered.at[p, c, pl.ds(pl.multiple_of(me * rows, rows), rows), :],
            send_sem=gather_send.at[p, c, off],
            recv_sem=gather_recv.at[p, c, off],
            device_id={"tensor": lax.rem(me + off, tensor_count)},
            device_id_type=MESH,
        )

    def next_copy(p, c, off):
        return pltpu.make_async_remote_copy(
            src_ref=hidden_low.at[p, c],
            dst_ref=gathered.at[p, c, pl.ds(pl.multiple_of(me * rows, rows), rows), :],
            send_sem=next_send.at[p, c, off],
            recv_sem=gather_recv.at[p, c, off],
            device_id={"tensor": lax.rem(me + off, tensor_count), "section": 1},
            device_id_type=MESH,
        )

    def wide(row):
        return jnp.concatenate([row] * (part // length), axis=1) if part > length else row[:, :part]

    @pl.when(section == 0)
    def _():
        @pl.loop(0, CHUNKS)
        def _(c):
            columns = pl.ds(pl.multiple_of(c * part, part), part)

            def choose(target):
                total = jnp.zeros((rows, part), jnp.float32)
                for k in range(micro):
                    wanted = jnp.zeros((1, length), jnp.float32)
                    for i in range(micro):
                        row = meta[target, micro + i : micro + i + 1, :]
                        wanted = wanted + jnp.where(row == z * micro + k, 1.0, 0.0)
                    total = total + tokens_ref[k, :, columns].astype(jnp.float32) * wide(wanted)
                return total.astype(jnp.bfloat16)

            held_packs[c, z] = choose(z)

            @pl.loop(1, dp_count)
            def _(off):
                target = lax.rem(z + off, dp_count)
                sent_packs[c, target] = choose(target)
                pack_copy(c, off).start()

    freq = frequency_ref[0:1, :]
    row_id = lax.broadcasted_iota(jnp.int32, (length, length), 0)
    column_id = lax.broadcasted_iota(jnp.int32, (length, length), 1)
    lane = lax.broadcasted_iota(jnp.int32, (length, HD), 1)
    for p in range(micro):
        own = meta[z, micro + p : micro + p + 1, :]

        def add_segment(holder, total, own=own):
            for k in range(micro):
                row = meta[holder, k : k + 1, :]
                total = total + jnp.where(own == holder * micro + k, row, 0)
            return total

        chosen = lax.fori_loop(0, dp_count, add_segment, jnp.zeros((1, length), jnp.int32))
        across = jnp.broadcast_to(chosen.astype(jnp.float32), (length, length))
        down = across.T
        earlier = jnp.sum(jnp.where(across < down, 1.0, 0.0), axis=1, keepdims=True)
        order = lax.broadcasted_iota(jnp.int32, (length, 1), 0).astype(jnp.float32)
        angle = (order - earlier) * freq
        cosine[p] = jnp.cos(angle)
        sine[p] = jnp.where(lane < HD // 2, -1.0, 1.0) * jnp.sin(angle)
        bias[p] = jnp.where((across == down) & (column_id <= row_id), 0.0, -1e30)

    @pl.when(section == 0)
    def _():
        @pl.loop(0, CHUNKS)
        def _(c):
            @pl.loop(1, dp_count)
            def _(off):
                pack_copy(c, off).wait_recv()

            for p in range(micro):
                own = meta[z, micro + p : micro + p + 1, :]

                def add_pack(holder, total, own=own):
                    hit = jnp.where((own >= holder * micro) & (own < (holder + 1) * micro), 1.0, 0.0)
                    return total + held_packs[c, holder].astype(jnp.float32) * wide(hit)

                picked = lax.fori_loop(
                    0, dp_count, add_pack, jnp.zeros((rows, part), jnp.float32)
                )
                hidden[p, c] = picked
                gathered[p, c, pl.ds(pl.multiple_of(me * rows, rows), rows), :] = picked.astype(
                    jnp.bfloat16
                )
                for off in range(1, tensor_count):
                    gather_copy(p, c, off).start()

    for copy in weight_copies:
        copy.wait()

    def sum_copy(p, c, off):
        target = lax.rem(me + off, tensor_count)
        place = c + section * (CHUNKS + c % half - c)
        return dict(
            src_ref=partial.at[p, c, pl.ds(pl.multiple_of(target * rows, rows), rows), :],
            dst_ref=arrived.at[p, place, me],
            to=(target, section * (c // half)),
            send_sem=sum_send.at[p, c, off],
            recv_sem=sum_recv.at[p, place, off],
        )

    def sum_remote(p, c, off):
        d = sum_copy(p, c, off)
        return pltpu.make_async_remote_copy(
            src_ref=d["src_ref"],
            dst_ref=d["dst_ref"],
            send_sem=d["send_sem"],
            recv_sem=d["recv_sem"],
            device_id={"tensor": d["to"][0], "section": d["to"][1]},
            device_id_type=MESH,
        )

    def rotate(x, p):
        return x * cosine[p] + pltpu.roll(x, HD // 2, 1) * sine[p]

    @pl.loop(0, micro)
    def _(p):
        @pl.loop(0, CHUNKS)
        def _(c):
            @pl.when(section == 1)
            def _():
                next_copy(p, c, 0).wait_recv()

            for off in range(1, tensor_count):
                gather_copy(p, c, off).wait_recv()
            block = gathered[p, c].astype(jnp.float32)
            squares = jnp.sum(block * block, axis=1, keepdims=True)
            normed[...] = (
                block * gain_ref[0:1, pl.ds(pl.multiple_of(c * part, part), part)]
            ).astype(jnp.bfloat16)
            total_columns = weight_in.shape[2]
            tile = 256

            @pl.when(c == 0)
            def _():
                square_sum[...] = jnp.broadcast_to(squares, square_sum.shape)
                for n in range(0, total_columns, tile):
                    projected[:, n : n + tile] = jnp.dot(
                        normed[...],
                        weight_in[c, :, n : n + tile],
                        preferred_element_type=jnp.float32,
                    )

            @pl.when(c > 0)
            def _():
                square_sum[...] += jnp.broadcast_to(squares, square_sum.shape)
                for n in range(0, total_columns, tile):
                    projected[:, n : n + tile] += jnp.dot(
                        normed[...],
                        weight_in[c, :, n : n + tile],
                        preferred_element_type=jnp.float32,
                    )

        scale = lax.rsqrt(square_sum[...] * (1.0 / width) + EPSILON)
        for g in range(groups):
            base = g * (GROUP + 2) * HD
            at = base + GROUP * HD
            key = rotate(projected[:, at : at + HD] * scale, p).astype(jnp.bfloat16)
            at = at + HD
            value = (projected[:, at : at + HD] * scale).astype(jnp.bfloat16)
            for h in range(GROUP):
                at = base + h * HD
                query = rotate(projected[:, at : at + HD] * scale, p).astype(jnp.bfloat16)
                scores = lax.dot_general(
                    query, key, (((1,), (1,)), ((), ())), preferred_element_type=jnp.float32
                )
                scores = jnp.where(bias[p] < 0.0, -1e30, scores * HD ** (-0.5))
                terms = jnp.exp(scores - jnp.max(scores, axis=1, keepdims=True))
                weights = (terms / jnp.sum(terms, axis=1, keepdims=True)).astype(jnp.bfloat16)
                at = (g * GROUP + h) * HD
                attended[:, at : at + HD] = jnp.dot(
                    weights, value, preferred_element_type=jnp.float32
                ).astype(jnp.bfloat16)

        @pl.loop(0, CHUNKS)
        def _(c):
            tile = min(256, part)
            for n in range(0, part, tile):
                partial[p, c, :, n : n + tile] = jnp.dot(
                    attended[...],
                    weight_out[c, :, n : n + tile],
                    preferred_element_type=jnp.float32,
                ).astype(jnp.bfloat16)
            for off in range(1, tensor_count):
                sum_remote(p, c, off).start()

            @pl.when(section * (c // half) == section)
            def _():
                d = sum_copy(p, c, 0)
                pltpu.make_async_copy(d["src_ref"], d["dst_ref"], d["recv_sem"]).start()

            @pl.when(section * (c // half) != section)
            def _():
                sum_remote(p, c, 0).start()

    def wait_sums(p, place):
        for off in range(tensor_count):
            pltpu.make_async_copy(
                arrived.at[p, place, lax.rem(me + tensor_count - off, tensor_count)],
                arrived.at[p, place, lax.rem(me + tensor_count - off, tensor_count)],
                sum_recv.at[p, place, off],
            ).wait()

    def add_up(p, place):
        total = arrived[p, place, 0].astype(jnp.float32)
        for t in range(1, tensor_count):
            total = total + arrived[p, place, t].astype(jnp.float32)
        return total

    @pl.when(section == 0)
    def _():
        @pl.loop(0, micro)
        def _(p):
            @pl.loop(0, CHUNKS)
            def _(c):
                wait_sums(p, c)
                after = hidden[p, c] + add_up(p, c)
                hidden[p, c] = after
                hidden_low[p, c] = after.astype(jnp.bfloat16)
                for off in range(tensor_count):
                    next_copy(p, c, off).start()

    @pl.when(section == 1)
    def _():
        for p in range(micro):
            for j in range(half):
                hidden[p, j] = gathered[
                    p, half + j, pl.ds(pl.multiple_of(me * rows, rows), rows), :
                ].astype(jnp.float32)

    @pl.loop(0, micro)
    def _(p):
        for j in range(half):
            wait_sums(p, CHUNKS + j)
            result_ref[p, :, j * part : (j + 1) * part] = (
                hidden[p, j] + add_up(p, CHUNKS + j)
            ).astype(jnp.bfloat16)

    @pl.loop(0, micro)
    def _(p):
        @pl.loop(0, CHUNKS)
        def _(c):
            for off in range(1, tensor_count):
                sum_remote(p, c, off).wait_send()

            @pl.when(section * (c // half) != section)
            def _():
                sum_remote(p, c, 0).wait_send()

            @pl.when(section == 0)
            def _():
                for off in range(1, tensor_count):
                    gather_copy(p, c, off).wait_send()
                for off in range(tensor_count):
                    next_copy(p, c, off).wait_send()

    @pl.when(section == 0)
    def _():
        @pl.loop(0, CHUNKS)
        def _(c):
            @pl.loop(1, dp_count)
            def _(off):
                pack_copy(c, off).wait_send()


def on_device(tokens, segment, pack_source, norm_gain, qkv_weight, out_weight):
    dp_count = lax.axis_size("dp")
    tensor_count = lax.axis_size("tensor")
    micro, rows, width = tokens.shape
    length = segment.shape[1]
    part = width // CHUNKS
    columns = qkv_weight.shape[2]
    depth = out_weight.shape[1]
    places = CHUNKS + CHUNKS // 2
    exponent = jnp.arange(0, HD, 2, dtype=jnp.float32) / HD
    frequency = ROPE_BASE ** (-exponent)
    frequency = jnp.concatenate([frequency, frequency])[None, :]
    vmem = pl.BlockSpec(memory_space=pltpu.VMEM)
    anywhere = pl.BlockSpec(memory_space=pl.ANY)
    dma = pltpu.SemaphoreType.DMA
    bf16, f32 = jnp.bfloat16, jnp.float32
    return pl.pallas_call(
        functools.partial(kernel, dp_count, tensor_count),
        out_shape=jax.ShapeDtypeStruct((micro, rows, width // 2), bf16),
        in_specs=[
            vmem,
            pl.BlockSpec(memory_space=pltpu.SMEM),
            vmem,
            vmem,
            vmem,
            anywhere,
            anywhere,
        ],
        out_specs=vmem,
        scratch_shapes=[
            pltpu.VMEM((CHUNKS, part, columns), bf16),
            pltpu.VMEM((CHUNKS, depth, part), bf16),
            pltpu.VMEM((dp_count, 8, length), jnp.int32),
            pltpu.VMEM((CHUNKS, dp_count, rows, part), bf16),
            pltpu.VMEM((CHUNKS, dp_count, rows, part), bf16),
            pltpu.VMEM((micro, CHUNKS, length, part), bf16),
            pltpu.VMEM((micro, CHUNKS, rows, part), f32),
            pltpu.VMEM((micro, CHUNKS, rows, part), bf16),
            pltpu.VMEM((length, part), bf16),
            pltpu.VMEM((length, columns), f32),
            pltpu.VMEM((length, HD), f32),
            pltpu.VMEM((length, depth), bf16),
            pltpu.VMEM((micro, CHUNKS, length, part), bf16),
            pltpu.VMEM((micro, places, tensor_count, rows, part), bf16),
            pltpu.VMEM((micro, length, HD), f32),
            pltpu.VMEM((micro, length, HD), f32),
            pltpu.VMEM((micro, length, length), f32),
            dma((2 * CHUNKS,)),
            dma((dp_count,)),
            dma((dp_count,)),
            dma((CHUNKS, dp_count)),
            dma((CHUNKS, dp_count)),
            dma((micro, CHUNKS, tensor_count)),
            dma((micro, CHUNKS, tensor_count)),
            dma((micro, CHUNKS, tensor_count)),
            dma((micro, CHUNKS, tensor_count)),
            dma((micro, places, tensor_count)),
        ],
        compiler_params=pltpu.CompilerParams(
            collective_id=0, has_side_effects=True, vmem_limit_bytes=58 * 1024 * 1024
        ),
    )(frequency, pack_source, segment, tokens, norm_gain, qkv_weight, out_weight)


def solution(mesh):
    placed = (
        P("dp", "tensor", None),
        P("dp", None),
        P("dp"),
        P("section", None),
        P("section", None, "tensor"),
        P("section", "tensor", None),
    )
    return jax.shard_map(
        on_device,
        mesh=mesh,
        in_specs=placed,
        out_specs=P("dp", "tensor", "section"),
        check_vma=False,
    )
```

```python
import functools

import jax
import jax.numpy as jnp
from jax import lax
from jax.experimental import pallas as pl
from jax.experimental.pallas import tpu as pltpu
from jax.sharding import PartitionSpec as P

HD = 128
GROUP = 4
EPSILON = 1e-05
ROPE_BASE = 500000.0
CHUNKS = 4
MESH = pl.DeviceIdType.MESH


def kernel(
    dp_count,
    tensor_count,
    frequency_ref,
    source_ref,
    segment_ref,
    tokens_ref,
    gain_ref,
    qkv_hbm,
    out_hbm,
    result_ref,
    weight_in,
    weight_out,
    meta,
    sent_packs,
    held_packs,
    gathered,
    hidden,
    hidden_low,
    normed,
    projected,
    square_sum,
    attended,
    partial,
    arrived,
    cosine,
    sine,
    bias,
    weight_sem,
    meta_send,
    meta_recv,
    pack_send,
    pack_recv,
    gather_send,
    gather_recv,
    next_send,
    sum_send,
    sum_recv,
):
    micro, rows, width = tokens_ref.shape
    length = segment_ref.shape[1]
    part = width // CHUNKS
    half = CHUNKS // 2
    z = lax.axis_index("dp")
    section = lax.axis_index("section")
    me = lax.axis_index("tensor")
    groups = weight_in.shape[2] // ((GROUP + 2) * HD)

    weight_copies = [
        pltpu.make_async_copy(
            qkv_hbm.at[0, pl.ds(c * part, part), :], weight_in.at[c], weight_sem.at[c]
        )
        for c in range(CHUNKS)
    ] + [
        pltpu.make_async_copy(
            out_hbm.at[0, :, pl.ds(c * part, part)], weight_out.at[c], weight_sem.at[CHUNKS + c]
        )
        for c in range(CHUNKS)
    ]
    for copy in weight_copies:
        copy.start()

    for i in range(micro):
        meta[z, i : i + 1, :] = segment_ref[i : i + 1, :]
        meta[z, micro + i : micro + i + 1, :] = jnp.full((1, length), source_ref[i], jnp.int32)

    barrier = pltpu.get_barrier_semaphore()

    @pl.loop(1, dp_count)
    def _(off):
        pl.semaphore_signal(
            barrier, inc=1, device_id={"dp": lax.rem(z + off, dp_count)}, device_id_type=MESH
        )

    for off in range(tensor_count):
        for other in range(2):
            if off == 0 and other == 0:
                continue
            pl.semaphore_signal(
                barrier,
                inc=1,
                device_id={
                    "tensor": lax.rem(me + off, tensor_count),
                    "section": lax.rem(section + other, 2),
                },
                device_id_type=MESH,
            )
    pl.semaphore_wait(barrier, dp_count - 1 + 2 * tensor_count - 1)

    def meta_copy(off):
        return pltpu.make_async_remote_copy(
            src_ref=meta.at[z],
            dst_ref=meta.at[z],
            send_sem=meta_send.at[off],
            recv_sem=meta_recv.at[off],
            device_id={"dp": lax.rem(z + off, dp_count)},
            device_id_type=MESH,
        )

    @pl.loop(1, dp_count)
    def _(off):
        meta_copy(off).start()

    @pl.loop(1, dp_count)
    def _(off):
        copy = meta_copy(off)
        copy.wait_send()
        copy.wait_recv()

    def pack_copy(c, off):
        target = lax.rem(z + off, dp_count)
        return pltpu.make_async_remote_copy(
            src_ref=sent_packs.at[c, target],
            dst_ref=held_packs.at[c, z],
            send_sem=pack_send.at[c, off],
            recv_sem=pack_recv.at[c, off],
            device_id={"dp": target},
            device_id_type=MESH,
        )

    def gather_copy(p, c, off):
        return pltpu.make_async_remote_copy(
            src_ref=gathered.at[p, c, pl.ds(pl.multiple_of(me * rows, rows), rows), :],
            dst_ref=gathered.at[p, c, pl.ds(pl.multiple_of(me * rows, rows), rows), :],
            send_sem=gather_send.at[p, c, off],
            recv_sem=gather_recv.at[p, c, off],
            device_id={"tensor": lax.rem(me + off, tensor_count)},
            device_id_type=MESH,
        )

    def next_copy(p, c, off):
        return pltpu.make_async_remote_copy(
            src_ref=hidden_low.at[p, c],
            dst_ref=gathered.at[p, c, pl.ds(pl.multiple_of(me * rows, rows), rows), :],
            send_sem=next_send.at[p, c, off],
            recv_sem=gather_recv.at[p, c, off],
            device_id={"tensor": lax.rem(me + off, tensor_count), "section": 1},
            device_id_type=MESH,
        )

    def wide(row):
        return jnp.concatenate([row] * (part // length), axis=1) if part > length else row[:, :part]

    @pl.when(section == 0)
    def _():
        @pl.loop(0, CHUNKS)
        def _(c):
            columns = pl.ds(pl.multiple_of(c * part, part), part)

            def choose(target):
                total = jnp.zeros((rows, part), jnp.float32)
                for k in range(micro):
                    wanted = jnp.zeros((1, length), jnp.float32)
                    for i in range(micro):
                        row = meta[target, micro + i : micro + i + 1, :]
                        wanted = wanted + jnp.where(row == z * micro + k, 1.0, 0.0)
                    total = total + tokens_ref[k, :, columns].astype(jnp.float32) * wide(wanted)
                return total.astype(jnp.bfloat16)

            held_packs[c, z] = choose(z)

            @pl.loop(1, dp_count)
            def _(off):
                target = lax.rem(z + off, dp_count)
                sent_packs[c, target] = choose(target)
                pack_copy(c, off).start()

    freq = frequency_ref[0:1, :]
    row_id = lax.broadcasted_iota(jnp.int32, (length, length), 0)
    column_id = lax.broadcasted_iota(jnp.int32, (length, length), 1)
    lane = lax.broadcasted_iota(jnp.int32, (length, HD), 1)
    for p in range(micro):
        own = meta[z, micro + p : micro + p + 1, :]

        def add_segment(holder, total, own=own):
            for k in range(micro):
                row = meta[holder, k : k + 1, :]
                total = total + jnp.where(own == holder * micro + k, row, 0)
            return total

        chosen = lax.fori_loop(0, dp_count, add_segment, jnp.zeros((1, length), jnp.int32))
        across = jnp.broadcast_to(chosen.astype(jnp.float32), (length, length))
        down = across.T
        earlier = jnp.sum(jnp.where(across < down, 1.0, 0.0), axis=1, keepdims=True)
        order = lax.broadcasted_iota(jnp.int32, (length, 1), 0).astype(jnp.float32)
        angle = (order - earlier) * freq
        cosine[p] = jnp.cos(angle)
        sine[p] = jnp.where(lane < HD // 2, -1.0, 1.0) * jnp.sin(angle)
        bias[p] = jnp.where((across == down) & (column_id <= row_id), 0.0, -1e30)

    @pl.when(section == 0)
    def _():
        @pl.loop(0, CHUNKS)
        def _(c):
            @pl.loop(1, dp_count)
            def _(off):
                pack_copy(c, off).wait_recv()

            for p in range(micro):
                own = meta[z, micro + p : micro + p + 1, :]

                def add_pack(holder, total, own=own):
                    hit = jnp.where((own >= holder * micro) & (own < (holder + 1) * micro), 1.0, 0.0)
                    return total + held_packs[c, holder].astype(jnp.float32) * wide(hit)

                picked = lax.fori_loop(
                    0, dp_count, add_pack, jnp.zeros((rows, part), jnp.float32)
                )
                hidden[p, c] = picked
                gathered[p, c, pl.ds(pl.multiple_of(me * rows, rows), rows), :] = picked.astype(
                    jnp.bfloat16
                )
                for off in range(1, tensor_count):
                    gather_copy(p, c, off).start()

    for copy in weight_copies:
        copy.wait()

    def sum_copy(p, c, off):
        target = lax.rem(me + off, tensor_count)
        place = c + section * (CHUNKS + c % half - c)
        return dict(
            src_ref=partial.at[p, c, pl.ds(pl.multiple_of(target * rows, rows), rows), :],
            dst_ref=arrived.at[p, place, me],
            to=(target, section * (c // half)),
            send_sem=sum_send.at[p, c, off],
            recv_sem=sum_recv.at[p, place, off],
        )

    def sum_remote(p, c, off):
        d = sum_copy(p, c, off)
        return pltpu.make_async_remote_copy(
            src_ref=d["src_ref"],
            dst_ref=d["dst_ref"],
            send_sem=d["send_sem"],
            recv_sem=d["recv_sem"],
            device_id={"tensor": d["to"][0], "section": d["to"][1]},
            device_id_type=MESH,
        )

    def rotate(x, p):
        return x * cosine[p] + pltpu.roll(x, HD // 2, 1) * sine[p]

    @pl.loop(0, micro)
    def _(p):
        @pl.loop(0, CHUNKS)
        def _(c):
            @pl.when(section == 1)
            def _():
                next_copy(p, c, 0).wait_recv()

            for off in range(1, tensor_count):
                gather_copy(p, c, off).wait_recv()
            block = gathered[p, c].astype(jnp.float32)
            squares = jnp.sum(block * block, axis=1, keepdims=True)
            normed[...] = (
                block * gain_ref[0:1, pl.ds(pl.multiple_of(c * part, part), part)]
            ).astype(jnp.bfloat16)
            total_columns = weight_in.shape[2]
            tile = 256

            @pl.when(c == 0)
            def _():
                square_sum[...] = jnp.broadcast_to(squares, square_sum.shape)
                for n in range(0, total_columns, tile):
                    projected[:, n : n + tile] = jnp.dot(
                        normed[...],
                        weight_in[c, :, n : n + tile],
                        preferred_element_type=jnp.float32,
                    )

            @pl.when(c > 0)
            def _():
                square_sum[...] += jnp.broadcast_to(squares, square_sum.shape)
                for n in range(0, total_columns, tile):
                    projected[:, n : n + tile] += jnp.dot(
                        normed[...],
                        weight_in[c, :, n : n + tile],
                        preferred_element_type=jnp.float32,
                    )

        scale = lax.rsqrt(square_sum[...] * (1.0 / width) + EPSILON)
        for g in range(groups):
            base = g * (GROUP + 2) * HD
            at = base + GROUP * HD
            key = rotate(projected[:, at : at + HD] * scale, p).astype(jnp.bfloat16)
            at = at + HD
            value = (projected[:, at : at + HD] * scale).astype(jnp.bfloat16)
            queries = jnp.concatenate(
                [
                    rotate(
                        projected[:, base + h * HD : base + (h + 1) * HD] * scale, p
                    ).astype(jnp.bfloat16)
                    for h in range(GROUP)
                ],
                axis=0,
            )
            scores = lax.dot_general(
                queries, key, (((1,), (1,)), ((), ())), preferred_element_type=jnp.float32
            )
            masked = jnp.concatenate([bias[p]] * GROUP, axis=0)
            scores = jnp.where(masked < 0.0, -1e30, scores * HD ** (-0.5))
            terms = jnp.exp(scores - jnp.max(scores, axis=1, keepdims=True))
            weights = (terms * (1.0 / jnp.sum(terms, axis=1, keepdims=True))).astype(jnp.bfloat16)
            mixed = jnp.dot(weights, value, preferred_element_type=jnp.float32)
            for h in range(GROUP):
                at = (g * GROUP + h) * HD
                attended[:, at : at + HD] = mixed[h * length : (h + 1) * length, :].astype(
                    jnp.bfloat16
                )

        @pl.loop(0, CHUNKS)
        def _(c):
            tile = min(256, part)
            for n in range(0, part, tile):
                partial[p, c, :, n : n + tile] = jnp.dot(
                    attended[...],
                    weight_out[c, :, n : n + tile],
                    preferred_element_type=jnp.float32,
                ).astype(jnp.bfloat16)
            for off in range(1, tensor_count):
                sum_remote(p, c, off).start()

            @pl.when(section * (c // half) == section)
            def _():
                d = sum_copy(p, c, 0)
                pltpu.make_async_copy(d["src_ref"], d["dst_ref"], d["recv_sem"]).start()

            @pl.when(section * (c // half) != section)
            def _():
                sum_remote(p, c, 0).start()

    def wait_sums(p, place):
        for off in range(tensor_count):
            pltpu.make_async_copy(
                arrived.at[p, place, lax.rem(me + tensor_count - off, tensor_count)],
                arrived.at[p, place, lax.rem(me + tensor_count - off, tensor_count)],
                sum_recv.at[p, place, off],
            ).wait()

    def add_up(p, place):
        total = arrived[p, place, 0].astype(jnp.float32)
        for t in range(1, tensor_count):
            total = total + arrived[p, place, t].astype(jnp.float32)
        return total

    @pl.when(section == 0)
    def _():
        @pl.loop(0, micro)
        def _(p):
            @pl.loop(0, CHUNKS)
            def _(c):
                wait_sums(p, c)
                after = hidden[p, c] + add_up(p, c)
                hidden[p, c] = after
                hidden_low[p, c] = after.astype(jnp.bfloat16)
                for off in range(tensor_count):
                    next_copy(p, c, off).start()

    @pl.when(section == 1)
    def _():
        for p in range(micro):
            for j in range(half):
                hidden[p, j] = gathered[
                    p, half + j, pl.ds(pl.multiple_of(me * rows, rows), rows), :
                ].astype(jnp.float32)

    @pl.loop(0, micro)
    def _(p):
        for j in range(half):
            wait_sums(p, CHUNKS + j)
            result_ref[p, :, j * part : (j + 1) * part] = (
                hidden[p, j] + add_up(p, CHUNKS + j)
            ).astype(jnp.bfloat16)

    @pl.loop(0, micro)
    def _(p):
        @pl.loop(0, CHUNKS)
        def _(c):
            for off in range(1, tensor_count):
                sum_remote(p, c, off).wait_send()

            @pl.when(section * (c // half) != section)
            def _():
                sum_remote(p, c, 0).wait_send()

            @pl.when(section == 0)
            def _():
                for off in range(1, tensor_count):
                    gather_copy(p, c, off).wait_send()
                for off in range(tensor_count):
                    next_copy(p, c, off).wait_send()

    @pl.when(section == 0)
    def _():
        @pl.loop(0, CHUNKS)
        def _(c):
            @pl.loop(1, dp_count)
            def _(off):
                pack_copy(c, off).wait_send()


def on_device(tokens, segment, pack_source, norm_gain, qkv_weight, out_weight):
    dp_count = lax.axis_size("dp")
    tensor_count = lax.axis_size("tensor")
    micro, rows, width = tokens.shape
    length = segment.shape[1]
    part = width // CHUNKS
    columns = qkv_weight.shape[2]
    depth = out_weight.shape[1]
    places = CHUNKS + CHUNKS // 2
    exponent = jnp.arange(0, HD, 2, dtype=jnp.float32) / HD
    frequency = ROPE_BASE ** (-exponent)
    frequency = jnp.concatenate([frequency, frequency])[None, :]
    vmem = pl.BlockSpec(memory_space=pltpu.VMEM)
    anywhere = pl.BlockSpec(memory_space=pl.ANY)
    dma = pltpu.SemaphoreType.DMA
    bf16, f32 = jnp.bfloat16, jnp.float32
    return pl.pallas_call(
        functools.partial(kernel, dp_count, tensor_count),
        out_shape=jax.ShapeDtypeStruct((micro, rows, width // 2), bf16),
        in_specs=[
            vmem,
            pl.BlockSpec(memory_space=pltpu.SMEM),
            vmem,
            vmem,
            vmem,
            anywhere,
            anywhere,
        ],
        out_specs=vmem,
        scratch_shapes=[
            pltpu.VMEM((CHUNKS, part, columns), bf16),
            pltpu.VMEM((CHUNKS, depth, part), bf16),
            pltpu.VMEM((dp_count, 8, length), jnp.int32),
            pltpu.VMEM((CHUNKS, dp_count, rows, part), bf16),
            pltpu.VMEM((CHUNKS, dp_count, rows, part), bf16),
            pltpu.VMEM((micro, CHUNKS, length, part), bf16),
            pltpu.VMEM((micro, CHUNKS, rows, part), f32),
            pltpu.VMEM((micro, CHUNKS, rows, part), bf16),
            pltpu.VMEM((length, part), bf16),
            pltpu.VMEM((length, columns), f32),
            pltpu.VMEM((length, HD), f32),
            pltpu.VMEM((length, depth), bf16),
            pltpu.VMEM((micro, CHUNKS, length, part), bf16),
            pltpu.VMEM((micro, places, tensor_count, rows, part), bf16),
            pltpu.VMEM((micro, length, HD), f32),
            pltpu.VMEM((micro, length, HD), f32),
            pltpu.VMEM((micro, length, length), f32),
            dma((2 * CHUNKS,)),
            dma((dp_count,)),
            dma((dp_count,)),
            dma((CHUNKS, dp_count)),
            dma((CHUNKS, dp_count)),
            dma((micro, CHUNKS, tensor_count)),
            dma((micro, CHUNKS, tensor_count)),
            dma((micro, CHUNKS, tensor_count)),
            dma((micro, CHUNKS, tensor_count)),
            dma((micro, places, tensor_count)),
        ],
        compiler_params=pltpu.CompilerParams(
            collective_id=0, has_side_effects=True, vmem_limit_bytes=58 * 1024 * 1024
        ),
    )(frequency, pack_source, segment, tokens, norm_gain, qkv_weight, out_weight)


def solution(mesh):
    placed = (
        P("dp", "tensor", None),
        P("dp", None),
        P("dp"),
        P("section", None),
        P("section", None, "tensor"),
        P("section", "tensor", None),
    )
    return jax.shard_map(
        on_device,
        mesh=mesh,
        in_specs=placed,
        out_specs=P("dp", "tensor", "section"),
        check_vma=False,
    )
```

```python
import functools
import math

import jax
import jax.numpy as jnp
from jax import lax
from jax.experimental import pallas as pl
from jax.experimental.pallas import tpu as pltpu
from jax.sharding import PartitionSpec as P

HD = 128
GROUP = 4
EPSILON = 1e-05
ROPE_BASE = 500000.0
CHUNKS = 4
MESH = pl.DeviceIdType.MESH


def kernel(
    dp_count,
    tensor_count,
    source_ref,
    segment_ref,
    tokens_ref,
    gain_ref,
    qkv_hbm,
    out_hbm,
    result_ref,
    weight_in,
    weight_out,
    meta,
    sent_packs,
    held_packs,
    gathered,
    hidden,
    hidden_low,
    normed,
    projected,
    square_sum,
    attended,
    partial,
    arrived,
    cosine,
    sine,
    bias,
    weight_sem,
    meta_send,
    meta_recv,
    pack_send,
    pack_recv,
    gather_send,
    gather_recv,
    next_send,
    sum_send,
    sum_recv,
):
    micro, rows, width = tokens_ref.shape
    length = segment_ref.shape[1]
    part = width // CHUNKS
    half = CHUNKS // 2
    z = lax.axis_index("dp")
    section = lax.axis_index("section")
    me = lax.axis_index("tensor")
    groups = weight_in.shape[2] // ((GROUP + 2) * HD)

    weight_copies = [
        pltpu.make_async_copy(
            qkv_hbm.at[0, pl.ds(c * part, part), :], weight_in.at[c], weight_sem.at[c]
        )
        for c in range(CHUNKS)
    ] + [
        pltpu.make_async_copy(
            out_hbm.at[0, :, pl.ds(c * part, part)], weight_out.at[c], weight_sem.at[CHUNKS + c]
        )
        for c in range(CHUNKS)
    ]
    for copy in weight_copies:
        copy.start()

    for i in range(micro):
        meta[z, i : i + 1, :] = segment_ref[i : i + 1, :]
        meta[z, micro + i : micro + i + 1, :] = jnp.full((1, length), source_ref[i], jnp.int32)

    barrier = pltpu.get_barrier_semaphore()

    @pl.loop(1, dp_count)
    def _(off):
        pl.semaphore_signal(
            barrier, inc=1, device_id={"dp": lax.rem(z + off, dp_count)}, device_id_type=MESH
        )

    for off in range(tensor_count):
        for other in range(2):
            if off == 0 and other == 0:
                continue
            pl.semaphore_signal(
                barrier,
                inc=1,
                device_id={
                    "tensor": lax.rem(me + off, tensor_count),
                    "section": lax.rem(section + other, 2),
                },
                device_id_type=MESH,
            )
    pl.semaphore_wait(barrier, dp_count - 1 + 2 * tensor_count - 1)

    def meta_copy(off):
        return pltpu.make_async_remote_copy(
            src_ref=meta.at[z],
            dst_ref=meta.at[z],
            send_sem=meta_send.at[off],
            recv_sem=meta_recv.at[off],
            device_id={"dp": lax.rem(z + off, dp_count)},
            device_id_type=MESH,
        )

    @pl.loop(1, dp_count)
    def _(off):
        meta_copy(off).start()

    @pl.loop(1, dp_count)
    def _(off):
        copy = meta_copy(off)
        copy.wait_send()
        copy.wait_recv()

    def pack_copy(c, off):
        target = lax.rem(z + off, dp_count)
        return pltpu.make_async_remote_copy(
            src_ref=sent_packs.at[c, target],
            dst_ref=held_packs.at[c, z],
            send_sem=pack_send.at[c, off],
            recv_sem=pack_recv.at[c, off],
            device_id={"dp": target},
            device_id_type=MESH,
        )

    def gather_copy(p, c, off):
        return pltpu.make_async_remote_copy(
            src_ref=gathered.at[p, c, pl.ds(pl.multiple_of(me * rows, rows), rows), :],
            dst_ref=gathered.at[p, c, pl.ds(pl.multiple_of(me * rows, rows), rows), :],
            send_sem=gather_send.at[p, c, off],
            recv_sem=gather_recv.at[p, c, off],
            device_id={"tensor": lax.rem(me + off, tensor_count)},
            device_id_type=MESH,
        )

    def next_copy(p, c, off):
        return pltpu.make_async_remote_copy(
            src_ref=hidden_low.at[p, c],
            dst_ref=gathered.at[p, c, pl.ds(pl.multiple_of(me * rows, rows), rows), :],
            send_sem=next_send.at[p, c, off],
            recv_sem=gather_recv.at[p, c, off],
            device_id={"tensor": lax.rem(me + off, tensor_count), "section": 1},
            device_id_type=MESH,
        )

    def wide(row):
        return jnp.concatenate([row] * (part // length), axis=1) if part > length else row[:, :part]

    @pl.when(section == 0)
    def _():
        @pl.loop(0, CHUNKS)
        def _(c):
            columns = pl.ds(pl.multiple_of(c * part, part), part)

            def choose(target):
                total = jnp.zeros((rows, part), jnp.float32)
                for k in range(micro):
                    wanted = jnp.zeros((1, length), jnp.float32)
                    for i in range(micro):
                        row = meta[target, micro + i : micro + i + 1, :]
                        wanted = wanted + jnp.where(row == z * micro + k, 1.0, 0.0)
                    total = total + tokens_ref[k, :, columns].astype(jnp.float32) * wide(wanted)
                return total.astype(jnp.bfloat16)

            held_packs[c, z] = choose(z)

            @pl.loop(1, dp_count)
            def _(off):
                target = lax.rem(z + off, dp_count)
                sent_packs[c, target] = choose(target)
                pack_copy(c, off).start()

    row_id = lax.broadcasted_iota(jnp.int32, (length, length), 0)
    column_id = lax.broadcasted_iota(jnp.int32, (length, length), 1)
    lane = lax.broadcasted_iota(jnp.int32, (length, HD), 1)
    pair = (lax.broadcasted_iota(jnp.int32, (1, HD), 1) % (HD // 2)).astype(jnp.float32)
    freq = jnp.exp(pair * (-2.0 * math.log(ROPE_BASE) / HD))
    for p in range(micro):
        own = meta[z, micro + p : micro + p + 1, :]

        def add_segment(holder, total, own=own):
            for k in range(micro):
                row = meta[holder, k : k + 1, :]
                total = total + jnp.where(own == holder * micro + k, row, 0)
            return total

        chosen = lax.fori_loop(0, dp_count, add_segment, jnp.zeros((1, length), jnp.int32))
        across = jnp.broadcast_to(chosen.astype(jnp.float32), (length, length))
        down = across.T
        earlier = jnp.sum(jnp.where(across < down, 1.0, 0.0), axis=1, keepdims=True)
        order = lax.broadcasted_iota(jnp.int32, (length, 1), 0).astype(jnp.float32)
        angle = (order - earlier) * freq
        cosine[p] = jnp.cos(angle)
        sine[p] = jnp.where(lane < HD // 2, -1.0, 1.0) * jnp.sin(angle)
        bias[p] = jnp.where((across == down) & (column_id <= row_id), 0.0, -1e30)

    @pl.when(section == 0)
    def _():
        @pl.loop(0, CHUNKS)
        def _(c):
            @pl.loop(1, dp_count)
            def _(off):
                pack_copy(c, off).wait_recv()

            for p in range(micro):
                own = meta[z, micro + p : micro + p + 1, :]

                def add_pack(holder, total, own=own):
                    hit = jnp.where((own >= holder * micro) & (own < (holder + 1) * micro), 1.0, 0.0)
                    return total + held_packs[c, holder].astype(jnp.float32) * wide(hit)

                picked = lax.fori_loop(
                    0, dp_count, add_pack, jnp.zeros((rows, part), jnp.float32)
                )
                hidden[p, c] = picked
                gathered[p, c, pl.ds(pl.multiple_of(me * rows, rows), rows), :] = picked.astype(
                    jnp.bfloat16
                )
                for off in range(tensor_count - 1, 0, -1):
                    gather_copy(p, c, off).start()

    for copy in weight_copies:
        copy.wait()

    def sum_copy(p, c, off):
        target = lax.rem(me + off, tensor_count)
        place = c + section * (CHUNKS + c % half - c)
        return dict(
            src_ref=partial.at[p, c, pl.ds(pl.multiple_of(target * rows, rows), rows), :],
            dst_ref=arrived.at[p, place, me],
            to=(target, section * (c // half)),
            send_sem=sum_send.at[p, c, off],
            recv_sem=sum_recv.at[p, place, off],
        )

    def sum_remote(p, c, off):
        d = sum_copy(p, c, off)
        return pltpu.make_async_remote_copy(
            src_ref=d["src_ref"],
            dst_ref=d["dst_ref"],
            send_sem=d["send_sem"],
            recv_sem=d["recv_sem"],
            device_id={"tensor": d["to"][0], "section": d["to"][1]},
            device_id_type=MESH,
        )

    def rotate(x, p):
        return x * cosine[p] + pltpu.roll(x, HD // 2, 1) * sine[p]

    @pl.loop(0, micro)
    def _(p):
        @pl.loop(0, CHUNKS)
        def _(c):
            @pl.when(section == 1)
            def _():
                next_copy(p, c, 0).wait_recv()

            for off in range(tensor_count - 1, 0, -1):
                gather_copy(p, c, off).wait_recv()
            block = gathered[p, c].astype(jnp.float32)
            squares = jnp.sum(block * block, axis=1, keepdims=True)
            normed[...] = (
                block * gain_ref[0:1, pl.ds(pl.multiple_of(c * part, part), part)]
            ).astype(jnp.bfloat16)
            total_columns = weight_in.shape[2]
            tile = 256

            @pl.when(c == 0)
            def _():
                square_sum[...] = jnp.broadcast_to(squares, square_sum.shape)
                for n in range(0, total_columns, tile):
                    projected[:, n : n + tile] = jnp.dot(
                        normed[...],
                        weight_in[c, :, n : n + tile],
                        preferred_element_type=jnp.float32,
                    )

            @pl.when(c > 0)
            def _():
                square_sum[...] += jnp.broadcast_to(squares, square_sum.shape)
                for n in range(0, total_columns, tile):
                    projected[:, n : n + tile] += jnp.dot(
                        normed[...],
                        weight_in[c, :, n : n + tile],
                        preferred_element_type=jnp.float32,
                    )

        scale = lax.rsqrt(square_sum[...] * (1.0 / width) + EPSILON)
        for g in range(groups):
            base = g * (GROUP + 2) * HD
            at = base + GROUP * HD
            key = rotate(projected[:, at : at + HD] * scale, p).astype(jnp.bfloat16)
            at = at + HD
            value = (projected[:, at : at + HD] * scale).astype(jnp.bfloat16)
            queries = jnp.concatenate(
                [
                    rotate(
                        projected[:, base + h * HD : base + (h + 1) * HD] * scale, p
                    ).astype(jnp.bfloat16)
                    for h in range(GROUP)
                ],
                axis=0,
            )
            scores = lax.dot_general(
                queries, key, (((1,), (1,)), ((), ())), preferred_element_type=jnp.float32
            )
            masked = jnp.concatenate([bias[p]] * GROUP, axis=0)
            scores = jnp.where(masked < 0.0, -1e30, scores * HD ** (-0.5))
            terms = jnp.exp(scores - jnp.max(scores, axis=1, keepdims=True))
            weights = (terms * (1.0 / jnp.sum(terms, axis=1, keepdims=True))).astype(jnp.bfloat16)
            mixed = jnp.dot(weights, value, preferred_element_type=jnp.float32)
            for h in range(GROUP):
                at = (g * GROUP + h) * HD
                attended[:, at : at + HD] = mixed[h * length : (h + 1) * length, :].astype(
                    jnp.bfloat16
                )

        @pl.loop(0, CHUNKS)
        def _(c):
            tile = min(256, part)
            for n in range(0, part, tile):
                partial[p, c, :, n : n + tile] = jnp.dot(
                    attended[...],
                    weight_out[c, :, n : n + tile],
                    preferred_element_type=jnp.float32,
                ).astype(jnp.bfloat16)
            for off in range(tensor_count - 1, 0, -1):
                sum_remote(p, c, off).start()

            @pl.when(section * (c // half) == section)
            def _():
                d = sum_copy(p, c, 0)
                pltpu.make_async_copy(d["src_ref"], d["dst_ref"], d["recv_sem"]).start()

            @pl.when(section * (c // half) != section)
            def _():
                sum_remote(p, c, 0).start()

    def wait_sums(p, place):
        for off in range(tensor_count):
            pltpu.make_async_copy(
                arrived.at[p, place, lax.rem(me + tensor_count - off, tensor_count)],
                arrived.at[p, place, lax.rem(me + tensor_count - off, tensor_count)],
                sum_recv.at[p, place, off],
            ).wait()

    def add_up(p, place):
        total = arrived[p, place, 0].astype(jnp.float32)
        for t in range(1, tensor_count):
            total = total + arrived[p, place, t].astype(jnp.float32)
        return total

    @pl.when(section == 0)
    def _():
        @pl.loop(0, micro)
        def _(p):
            @pl.loop(0, CHUNKS)
            def _(c):
                wait_sums(p, c)
                after = hidden[p, c] + add_up(p, c)
                hidden[p, c] = after
                hidden_low[p, c] = after.astype(jnp.bfloat16)
                for off in range(tensor_count - 1, -1, -1):
                    next_copy(p, c, off).start()

    @pl.when(section == 1)
    def _():
        for p in range(micro):
            for j in range(half):
                hidden[p, j] = gathered[
                    p, half + j, pl.ds(pl.multiple_of(me * rows, rows), rows), :
                ].astype(jnp.float32)

    @pl.loop(0, micro)
    def _(p):
        for j in range(half):
            wait_sums(p, CHUNKS + j)
            result_ref[p, :, j * part : (j + 1) * part] = (
                hidden[p, j] + add_up(p, CHUNKS + j)
            ).astype(jnp.bfloat16)

    @pl.loop(0, micro)
    def _(p):
        @pl.loop(0, CHUNKS)
        def _(c):
            for off in range(tensor_count - 1, 0, -1):
                sum_remote(p, c, off).wait_send()

            @pl.when(section * (c // half) != section)
            def _():
                sum_remote(p, c, 0).wait_send()

            @pl.when(section == 0)
            def _():
                for off in range(tensor_count - 1, 0, -1):
                    gather_copy(p, c, off).wait_send()
                for off in range(tensor_count - 1, -1, -1):
                    next_copy(p, c, off).wait_send()

    @pl.when(section == 0)
    def _():
        @pl.loop(0, CHUNKS)
        def _(c):
            @pl.loop(1, dp_count)
            def _(off):
                pack_copy(c, off).wait_send()


def on_device(tokens, segment, pack_source, norm_gain, qkv_weight, out_weight):
    dp_count = lax.axis_size("dp")
    tensor_count = lax.axis_size("tensor")
    micro, rows, width = tokens.shape
    length = segment.shape[1]
    part = width // CHUNKS
    columns = qkv_weight.shape[2]
    depth = out_weight.shape[1]
    places = CHUNKS + CHUNKS // 2
    vmem = pl.BlockSpec(memory_space=pltpu.VMEM)
    anywhere = pl.BlockSpec(memory_space=pl.ANY)
    dma = pltpu.SemaphoreType.DMA
    bf16, f32 = jnp.bfloat16, jnp.float32
    return pl.pallas_call(
        functools.partial(kernel, dp_count, tensor_count),
        out_shape=jax.ShapeDtypeStruct((micro, rows, width // 2), bf16),
        in_specs=[
            pl.BlockSpec(memory_space=pltpu.SMEM),
            vmem,
            vmem,
            vmem,
            anywhere,
            anywhere,
        ],
        out_specs=vmem,
        scratch_shapes=[
            pltpu.VMEM((CHUNKS, part, columns), bf16),
            pltpu.VMEM((CHUNKS, depth, part), bf16),
            pltpu.VMEM((dp_count, 8, length), jnp.int32),
            pltpu.VMEM((CHUNKS, dp_count, rows, part), bf16),
            pltpu.VMEM((CHUNKS, dp_count, rows, part), bf16),
            pltpu.VMEM((micro, CHUNKS, length, part), bf16),
            pltpu.VMEM((micro, CHUNKS, rows, part), f32),
            pltpu.VMEM((micro, CHUNKS, rows, part), bf16),
            pltpu.VMEM((length, part), bf16),
            pltpu.VMEM((length, columns), f32),
            pltpu.VMEM((length, HD), f32),
            pltpu.VMEM((length, depth), bf16),
            pltpu.VMEM((micro, CHUNKS, length, part), bf16),
            pltpu.VMEM((micro, places, tensor_count, rows, part), bf16),
            pltpu.VMEM((micro, length, HD), f32),
            pltpu.VMEM((micro, length, HD), f32),
            pltpu.VMEM((micro, length, length), f32),
            dma((2 * CHUNKS,)),
            dma((dp_count,)),
            dma((dp_count,)),
            dma((CHUNKS, dp_count)),
            dma((CHUNKS, dp_count)),
            dma((micro, CHUNKS, tensor_count)),
            dma((micro, CHUNKS, tensor_count)),
            dma((micro, CHUNKS, tensor_count)),
            dma((micro, CHUNKS, tensor_count)),
            dma((micro, places, tensor_count)),
        ],
        compiler_params=pltpu.CompilerParams(
            collective_id=0, has_side_effects=True, vmem_limit_bytes=58 * 1024 * 1024
        ),
    )(pack_source, segment, tokens, norm_gain, qkv_weight, out_weight)


def solution(mesh):
    placed = (
        P("dp", "tensor", None),
        P("dp", None),
        P("dp"),
        P("section", None),
        P("section", None, "tensor"),
        P("section", "tensor", None),
    )
    return jax.shard_map(
        on_device,
        mesh=mesh,
        in_specs=placed,
        out_specs=P("dp", "tensor", "section"),
        check_vma=False,
    )
```
